1024 devices in a mesh: wave: 64 (over z, y), lev: 16 (over x, core).
Axes of the slice: x: 8, y: 8, z: 8, core: 2. Of those that a mesh axis runs over, the one named last changes fastest.
Arguments:
- spectra: float32 [640, 16, 3, 2, 1281], P('wave', 'lev'), may hold values from -0.005859375 to 0.005859375
- legendre: float32 [640, 64, 1281], P('wave'), may hold values from -4 to 4
- wave_table: int32 [640], replicated, may hold values from 0 to 639, each once
- lat_owner: int32 [64], replicated, may hold values from 0 to 63, as said below
- row_points: int32 [64], replicated, may hold values from 2580 to 5136, as said below
- weights: float32 [64], replicated, may hold values from 0.5 to 4
- layer_depth_factor: float32 [16], P('lev'), may hold values from 0.05 to 0.3
Outputs:
- spectral_out: float32 [640, 16, 3, 2, 1281], P('wave', 'lev')
- grid_terms: float32 [64, 16, 3, 5136], P('wave', 'lev')
The draws below stay inside these ranges and needn't reach their ends.
Inputs may be any that keep to these rules, and one draw needn't show every extreme that they name: `lat_owner`: each index of wave appears exactly 1 times. `row_points`: distinct and ascending, each equal to 20 + 4 i for a row number i; the first and last row numbers are always present.
All inputs are finite; a program needn't handle non-finite values.
Results may differ from the reference program's by a relative error of at most 0.0003.
Values sent between devices are 32-bit elements; how exact they have to be, the bound alone decides.
No kernel may reach another device: no remote copies, remote signals or barrier semaphores. Data moves between devices by JAX's collectives and lax.ppermute only.
A program may use at most 64 MiB of HBM per device.

```python
import math
import jax
import jax.numpy as jnp
from jax import lax

M = 1280
PAIRS = 640
SLOTS = 1281
LEV = 16
LAT_DEV = 1
NLAT = 64
ROW_FIRST = 640
ROW_LAST = 1279
PMAX = 5136


def draw_lat_owner(key, part):
    key = jax.random.fold_in(key, 7)
    shuffled = jax.random.permutation(key, NLAT)
    return (shuffled // LAT_DEV).astype(jnp.int32)


def draw_row_points(key, part):
    key = jax.random.fold_in(key, 11)
    middle = jax.random.permutation(key, ROW_LAST - ROW_FIRST - 1)[:NLAT - 2] + ROW_FIRST + 1
    numbers = jnp.concatenate([jnp.array([ROW_FIRST, ROW_LAST], jnp.int32), middle.astype(jnp.int32)])
    return (20 + 4 * jnp.sort(numbers)).astype(jnp.int32)


def level_of(key, shape, cuts, low, largest):
    def one(dim, shards_of):
        draws = jax.random.uniform(jax.random.fold_in(jax.random.fold_in(key, 6), dim), (shards_of,), jnp.float32, low / len(cuts), largest / len(cuts))
        return jnp.repeat(jnp.exp(draws), shape[dim] // shards_of).reshape((-1,) + (1,) * (len(shape) - dim - 1))

    loudness = one(*cuts[0])
    for cut in cuts[1:]:
        loudness = loudness * one(*cut)
    return loudness


def noise(own_key, dims, scale, limit, cuts=(), kind=jnp.bfloat16):
    result = scale * jax.random.normal(own_key, dims, jnp.float32)
    if cuts:
        result = result * level_of(own_key, dims, cuts, -0.22, 0.18)
    return jnp.clip(result, -limit, limit).astype(kind)


def setup_inputs(seed: int = 0) -> dict:
    arg_keys = jax.random.split(jax.random.key(seed), 8)
    return {
        "spectra": noise(arg_keys[0], (PAIRS, LEV, 3, 2, SLOTS), 0.001, 0.005859375, ((0, 64), (1, 16)), jnp.float32),
        "legendre": noise(arg_keys[1], (PAIRS, NLAT, SLOTS), 1.0, 4.0, ((0, 64),), jnp.float32),
        "wave_table": jax.random.permutation(arg_keys[2], PAIRS).astype(jnp.int32),
        "lat_owner": draw_lat_owner(jax.random.fold_in(arg_keys[7], 71), 0),
        "row_points": draw_row_points(jax.random.fold_in(arg_keys[7], 71), 0),
        "weights": jnp.clip(jnp.exp(jax.random.uniform(arg_keys[5], (NLAT,), jnp.float32, math.log(0.5), math.log(4.0))), 0.5, 4.0),
        "layer_depth_factor": jnp.clip(jnp.exp(math.log(0.3) - 1.7917595 * jax.random.uniform(arg_keys[6], (LEV,), jnp.float32) ** level_of(arg_keys[6], (LEV,), ((0, 16),), -0.2, 0.2)), 0.05, 0.3),
    }


def angles(length, wave_index, point_index):
    phase_index = (wave_index[:, None] * point_index[None, :]) % length
    angle_table = phase_index.astype(jnp.float32) * (2.0 * math.pi / length.astype(jnp.float32))
    inside = (point_index < length).astype(jnp.float32)
    return jnp.cos(angle_table), jnp.sin(angle_table), inside


def reference(spectra, legendre, wave_table, lat_owner, row_points, weights, layer_depth_factor):
    highest = lax.Precision.HIGHEST
    pair_count = M // 2
    columns = LEV * 6
    slot_index = jnp.arange(SLOTS, dtype=jnp.int32)
    lower_mask = (slot_index[None, :] < (M - wave_table)[:, None]).astype(jnp.float32)
    single_axis_view = spectra.reshape(pair_count, columns, SLOTS)

    def inverse_pair(packed):
        coeff_rows, basis_entries, mask_rows = packed
        stacked = jnp.concatenate([coeff_rows * mask_rows[None, :], coeff_rows * (1.0 - mask_rows)[None, :]], axis=0)
        return jnp.dot(stacked, basis_entries.T, precision=highest)

    fourier = lax.map(inverse_pair, (single_axis_view, legendre, lower_mask))
    fourier = fourier.reshape(pair_count * 2, columns, NLAT)
    wave_of = jnp.stack([wave_table, M - 1 - wave_table], axis=1).reshape(-1).astype(jnp.int32)
    by_wave = jnp.zeros((M, columns, NLAT), jnp.float32).at[wave_of].set(fourier)
    by_wave = by_wave.reshape(M, LEV * 3, 2, NLAT)
    factor = jnp.where(jnp.arange(M) == 0, 1.0, 2.0).astype(jnp.float32)
    real_part = jnp.transpose(by_wave[:, :, 0, :] * factor[:, None, None], (2, 0, 1))
    imag_part = jnp.transpose(by_wave[:, :, 1, :] * factor[:, None, None], (2, 0, 1))
    wave_index = jnp.arange(M, dtype=jnp.int32)
    point_index = jnp.arange(PMAX, dtype=jnp.int32)

    def synthesis(packed):
        real_row, imag_row, length = packed
        cosine_table, sine_table, inside = angles(length, wave_index, point_index)
        values = jnp.dot(real_row.T, cosine_table, precision=highest) - jnp.dot(imag_row.T, sine_table, precision=highest)
        return values * inside[None, :]

    physical_space_samples = lax.map(synthesis, (real_part, imag_part, row_points)).reshape(NLAT, LEV, 3, PMAX)
    zonal_velocity = physical_space_samples[:, :, 0]
    meridional_velocity = physical_space_samples[:, :, 1]
    thermal_state = physical_space_samples[:, :, 2]
    gaussian_scaled_samples = thermal_state * layer_depth_factor[None, :, None]
    geopotential = jnp.flip(jnp.cumsum(jnp.flip(gaussian_scaled_samples, 1), axis=1), 1)
    tendencies = jnp.stack([0.5 * (zonal_velocity * zonal_velocity + meridional_velocity * meridional_velocity) + geopotential,
                            zonal_velocity * thermal_state, meridional_velocity * thermal_state], axis=2)
    owner_order = jnp.argsort(lat_owner, stable=True).astype(jnp.int32)
    grid_terms = tendencies[owner_order]

    def analysis(packed):
        field_row, length = packed
        cosine_table, sine_table, inside = angles(length, wave_index, point_index)
        inverse_length = 1.0 / length.astype(jnp.float32)
        flat_row = field_row.reshape(LEV * 3, PMAX)
        real_out = jnp.dot(cosine_table, flat_row.T, precision=highest) * inverse_length
        imag_out = -jnp.dot(sine_table, flat_row.T, precision=highest) * inverse_length
        return jnp.stack([real_out, imag_out], axis=2)

    spectral_grid = lax.map(analysis, (tendencies, row_points))
    by_pair = spectral_grid[:, wave_of].reshape(NLAT, pair_count, 2, columns)
    by_pair = by_pair * weights[:, None, None, None]
    by_pair = jnp.transpose(by_pair, (1, 2, 3, 0))

    def direct_pair(packed):
        coeff_rows, basis_entries, mask_rows = packed
        lower_half = jnp.dot(coeff_rows[0], basis_entries, precision=highest)
        upper_half = jnp.dot(coeff_rows[1], basis_entries, precision=highest)
        return lower_half * mask_rows[None, :] + upper_half * (1.0 - mask_rows)[None, :]

    spectral_out = lax.map(direct_pair, (by_pair, legendre, lower_mask)).reshape(pair_count, LEV, 3, 2, SLOTS)
    return (spectral_out, grid_terms)
```

```python
import functools

import jax
import jax.numpy as jnp
from jax import lax
from jax.experimental import pallas as pl
from jax.experimental.pallas import tpu as pltpu
from jax.sharding import PartitionSpec as P

PMAX = 5136
QUARTER = 1408
COARSE = 80
FINE = 16
F32 = jnp.float32
BF16 = jnp.bfloat16
NN = (((1,), (0,)), ((), ()))
NT = (((1,), (1,)), ((), ()))

COS_POLY = (1.0, -19.73920440673828, 64.93911743164062, -85.45014190673828,
            60.16762924194336, -25.967599868774414, 6.528658390045166)
SIN_POLY = (6.2831854820251465, -41.34170150756836, 81.60513305664062, -76.70301818847656,
            42.02592849731445, -14.899847030639648, 3.2381374835968018)

SMEM = pl.BlockSpec(memory_space=pltpu.SMEM)
VMEM = pl.BlockSpec(memory_space=pltpu.VMEM)
HBM = pl.BlockSpec(memory_space=pl.ANY)


def split(x):
    hi = x.astype(BF16)
    return hi, (x - hi.astype(F32)).astype(BF16)


def dot(a, b, dims=NN):
    return lax.dot_general(a, b, dims, preferred_element_type=F32)


def iota(shape, axis):
    return lax.broadcasted_iota(jnp.int32, shape, axis)


def own_entry(owner_ref, table_ref, me, start):
    total = start
    for j in range(owner_ref.shape[0]):
        total = total + jnp.where(owner_ref[j] == me, table_ref[j], jnp.zeros_like(start))
    return total


SOURCE_ROWS = ((0, 4), (1, 0), (2, 2), (4, 5), (5, 1), (6, 3))


def legendre_kernel(wave, lev, pairs, wt_ref, factor_ref, spectra_ref, legendre_ref,
                    ft_ref, send_ref, xs_ref, xx_ref, lg_ref, t_ref, sem):
    me, level = wave(), lev()
    copies = [pltpu.make_async_copy(spectra_ref, xs_ref, sem.at[0])]
    for p in range(pairs):
        copies.append(pltpu.make_async_copy(legendre_ref.at[p], lg_ref.at[p], sem.at[1 + p]))
    for copy in copies:
        copy.start()
    ft_ref[...] = jnp.zeros_like(ft_ref)
    xx_ref[...] = jnp.zeros_like(xx_ref)
    t_ref[...] = jnp.zeros_like(t_ref)
    copies[0].wait()
    for p in range(pairs):
        for f in range(3):
            xx_ref[p, 2 * f:2 * f + 2, :] = xs_ref[p, 0, f, :, :]
    slots = xx_ref.shape[2]
    lane = iota((1, 128), 1)
    for p in range(pairs):
        bound = 1280 - wt_ref[me * pairs + p]
        x = xx_ref[p]
        low = iota(x.shape, 1) < bound
        s = jnp.concatenate([jnp.where(low, x, 0.0), jnp.where(low, 0.0, x)], axis=0)
        lhs = jnp.concatenate(split(s), axis=0)
        copies[1 + p].wait()
        rhs = jnp.concatenate(split(lg_ref[p]), axis=0)
        o = dot(lhs, rhs, NT)
        f = o[:16] + o[16:]
        f = f + pltpu.roll(f, 64, 1)
        for half in range(2):
            for to, source in SOURCE_ROWS:
                ft_ref[half, 8 * p + to:8 * p + to + 1, :] = f[8 * half + source:8 * half + source + 1]
            t_ref[pairs * half + p:pairs * half + p + 1, :] = jnp.where(
                lane < 64, f[8 * half + 4:8 * half + 5], f[8 * half + 5:8 * half + 6])
    thick = t_ref[...] * factor_ref[0]
    for k in range(send_ref.shape[0]):
        send_ref[k] = thick * jnp.where(k <= level, 1.0, 0.0).astype(F32)


def gather_kernel(pairs, owner_ref, ft_ref, recv_ref, send_ref, g_ref, f_ref, v_ref):
    g_ref[...] = jnp.sum(recv_ref[...], axis=0)
    for half in range(2):
        f_ref[half, 0:8 * pairs, :] = ft_ref[half]
        f_ref[half, 8 * pairs:, :] = jnp.zeros((128 - 8 * pairs, 128), F32)
        for p in range(pairs):
            row = g_ref[pairs * half + p:pairs * half + p + 1, :]
            f_ref[half, 8 * p + 3:8 * p + 4, :] = row
            f_ref[half, 8 * p + 7:8 * p + 8, :] = pltpu.roll(row, 64, 1)
        v_ref[half] = jnp.transpose(f_ref[half])
    for j in range(owner_ref.shape[0]):
        to = owner_ref[j]
        for half in range(2):
            send_ref[to, half:half + 1, :] = v_ref[half, j:j + 1, :]


def table_kernel(wave, owner_ref, points_ref, hi_ref, lo_ref, cos_ref, sin_ref):
    length = own_entry(owner_ref, points_ref, wave(), jnp.int32(0)).astype(F32)
    inverse = 1.0 / jnp.full((1, QUARTER), length, F32)
    point = iota((16, QUARTER), 1).astype(F32)
    row = iota((16, QUARTER), 0).astype(F32)

    def turn(wave_number):
        x = wave_number * point
        t = (x - jnp.floor(x * inverse + 0.5) * length) * inverse
        y = t * t
        c = jnp.full_like(y, COS_POLY[-1])
        s = jnp.full_like(y, SIN_POLY[-1])
        for a, b in zip(COS_POLY[-2::-1], SIN_POLY[-2::-1]):
            c = c * y + a
            s = s * y + b
        return c, s * t

    for i in range(COARSE // 16):
        c, s = turn((row + 16.0 * i) * FINE)
        at = pl.ds(16 * i, 16)
        hi_ref[at, :], lo_ref[at, :] = split(c)
        at = pl.ds(COARSE + 16 * i, 16)
        hi_ref[at, :], lo_ref[at, :] = split(s)
    c, s = turn(row)
    cos_ref[...] = c
    sin_ref[...] = s


def grid_kernel(wave, owner_ref, points_ref, weights_ref, order_ref, recv_ref, hi_ref, lo_ref,
                cos_ref, sin_ref, send_ref, terms_ref):
    me = wave()
    length = own_entry(owner_ref, points_ref, me, jnp.int32(0))
    weight = own_entry(owner_ref, weights_ref, me, jnp.float32(0))
    quarter = length // 4
    order = order_ref[...]
    fine = order & 15
    coarse = order >> 4
    a_row = iota((128, order.shape[1]), 0)
    pick = jnp.concatenate([
        jnp.where(coarse == a_row, 1.0, 0.0).astype(BF16),
        jnp.where(COARSE - 1 - coarse == a_row, 1.0, 0.0).astype(BF16)], axis=1)

    tops, lows = [], []
    for half in range(2):
        x = recv_ref[:, half, :]
        z = jnp.transpose(jnp.concatenate([x, pltpu.roll(x, 120, 1)], axis=0))
        xl = jnp.concatenate([z[16 * i:16 * i + 8] for i in range(5)], axis=1)
        hi = xl.astype(BF16).astype(F32)
        lo = xl - hi
        b_of = fine if half == 0 else FINE - 1 - fine
        tops.append(jnp.concatenate([jnp.where(b_of == b, hi, 0.0) for b in range(FINE)], axis=0).astype(BF16))
        lows.append(jnp.concatenate([jnp.where(b_of == b, lo, 0.0) for b in range(FINE)], axis=0).astype(BF16))
    lhs = jnp.concatenate([jnp.concatenate(tops, axis=1), jnp.concatenate(lows, axis=1)], axis=0)
    y = dot(lhs, pick, NT)
    y = y[:128] + y[128:]
    first = (iota((128, 128), 0) < 8) & (iota((128, 128), 1) == 0)
    y = y * jnp.where(first, 1.0, 2.0)
    in_real = (iota((128, 128), 0) & 7) < 4

    def swap(v):
        return pltpu.roll(v.reshape(FINE, 8, 128), 4, 1).reshape(128, 128)

    swapped = swap(y)
    lhs = jnp.concatenate([y, jnp.where(in_real, -swapped, swapped)], axis=1)
    lhs_hi, lhs_lo = split(lhs)
    lhs_both = jnp.concatenate([lhs_hi, lhs_lo], axis=0)

    acc = jnp.zeros((128, 256), F32)
    for start in range(0, QUARTER, 256):
        n = min(256, QUARTER - start)
        cols = slice(start, start + n)
        gap = jnp.zeros((48, n), BF16)
        t_hi = jnp.concatenate([hi_ref[0:80, cols], gap, hi_ref[80:160, cols], gap], axis=0)
        t_lo = jnp.concatenate([lo_ref[0:80, cols], gap, lo_ref[80:160, cols], gap], axis=0)
        part = dot(lhs_both, t_hi)
        part = part[:128] + part[128:] + dot(lhs_hi, t_lo)
        top = iota((8, n), 0) < 4
        turn_re, turn_im = [], []
        sums = {}

        def add(key, value):
            sums[key] = sums[key] + value if key in sums else value

        for b in range(FINE):
            c = jnp.broadcast_to(cos_ref[b:b + 1, cols], (8, n))
            s = jnp.broadcast_to(sin_ref[b:b + 1, cols], (8, n))
            turn_re.append(jnp.where(top, c, -s))
            turn_im.append(jnp.where(top, s, c) if b % 2 else None)
            rows = part[8 * b:8 * b + 8]
            add(("re", b % 4), rows * turn_re[b])
            if b % 2:
                add(("im", b % 4), rows * turn_im[b])

        def fold(v):
            return v + pltpu.roll(v, 4, 0)

        even_sum = fold(sums["re", 0] + sums["re", 2])
        even_dif = fold(sums["re", 0] - sums["re", 2])
        odd_sum = fold(sums["re", 1] + sums["re", 3])
        odd_dif = fold(sums["im", 3] - sums["im", 1])
        inside = iota((8, n), 1) + start < quarter
        kind = iota((8, n), 0) & 3
        terms = []
        for r, field in enumerate((even_sum + odd_sum, even_dif + odd_dif,
                                   even_sum - odd_sum, even_dif - odd_dif)):
            square = field * field
            energy = 0.5 * (pltpu.roll(square, 7, 0) + pltpu.roll(square, 6, 0)) + pltpu.roll(field, 5, 0)
            flux = field * field[0:1]
            value = jnp.where(kind == 0, energy, jnp.where(kind == 3, 0.0, flux))
            value = jnp.where(inside, value, 0.0)
            terms_ref[r, :, cols] = value
            terms.append(value)
        even, odd = terms[0] + terms[2], terms[1] + terms[3]
        real, imag = terms[0] - terms[2], terms[1] - terms[3]
        folded = {0: even + odd, 2: even - odd}
        back = []
        for b in range(FINE):
            if b % 2 == 0:
                back.append(folded[b % 4] * turn_re[b])
            elif b % 4 == 1:
                back.append(real * turn_re[b] - imag * turn_im[b])
            else:
                back.append(real * turn_re[b] + imag * turn_im[b])
        g_hi, g_lo = split(jnp.concatenate(back, axis=0))
        both = dot(jnp.concatenate([g_hi, g_lo], axis=0), t_hi, NT)
        acc = acc + both[:128] + both[128:] + dot(g_hi, t_lo, NT)

    swapped = swap(acc[:, 128:])
    analysed = acc[:, :128] + jnp.where(in_real, swapped, -swapped)
    analysed = analysed * (weight / jnp.full((1, 128), length.astype(F32), F32))

    a_hi, a_lo = split(analysed)
    v = dot(jnp.concatenate([a_hi, a_lo], axis=1), jnp.concatenate([pick, pick], axis=0))
    for half in range(2):
        b_of = fine if half == 0 else FINE - 1 - fine
        cols = slice(order.shape[1] * half, order.shape[1] * (half + 1))
        xl = jnp.zeros((8, order.shape[1]), F32)
        for b in range(FINE):
            xl = xl + jnp.where(b_of == b, v[8 * b:8 * b + 8, cols], 0.0)
        pieces = []
        for i in range(5):
            pieces += [xl[:, 128 * i:128 * i + 128], jnp.zeros((8, 128), F32)]
        z = jnp.transpose(jnp.concatenate(pieces + [jnp.zeros((48, 128), F32)], axis=0))
        send_ref[:, half, :] = z[:64] + pltpu.roll(z[64:], 8, 1)


def layout_kernel(wave, owner_ref, points_ref, terms_ref, out_ref, line_ref):
    quarter = own_entry(owner_ref, points_ref, wave(), jnp.int32(0)) // 4
    line_ref[...] = jnp.zeros_like(line_ref)
    gap = jnp.zeros((8, 128), F32)
    for r in range(4):
        at = r * quarter
        value = jnp.concatenate([terms_ref[r], gap], axis=1)
        value = pltpu.roll(value, at % 128, 1)
        where = pl.ds(pl.multiple_of(at // 128 * 128, 128), QUARTER + 128)
        line_ref[:, where] = line_ref[:, where] + value
    out_ref[0, 0, :, :] = line_ref[0:3, 0:PMAX]


def direct_kernel(wave, pairs, wt_ref, owner_ref, recv_ref, legendre_ref, out_ref, v_ref, lg_ref, sem):
    me = wave()
    copies = [pltpu.make_async_copy(legendre_ref.at[p], lg_ref.at[p], sem.at[p]) for p in range(pairs)]
    for copy in copies:
        copy.start()
    for j in range(owner_ref.shape[0]):
        source = owner_ref[j]
        for half in range(2):
            v_ref[half, j:j + 1, :] = recv_ref[source, half:half + 1, :]
    lane = iota((16, 128), 1)
    turned = [jnp.transpose(jnp.concatenate([v_ref[half], v_ref[half]], axis=0)) for half in range(2)]
    for p in range(pairs):
        bound = 1280 - wt_ref[me * pairs + p]
        q = jnp.concatenate([t[8 * p:8 * p + 8] for t in turned], axis=0)
        hi, lo = split(q)
        lhs = jnp.concatenate([hi, jnp.where(lane < 64, lo, jnp.zeros_like(lo))], axis=0)
        copies[p].wait()
        rhs = jnp.concatenate(split(lg_ref[p]), axis=0)
        o = dot(lhs, rhs)
        o = o[:16] + o[16:]
        y = jnp.where(iota((8, o.shape[1]), 1) < bound, o[:8], o[8:])
        for f in range(3):
            out_ref[p, 0, f, 0:1, :] = y[f:f + 1]
            out_ref[p, 0, f, 1:2, :] = y[4 + f:5 + f]


def params(megabytes=48):
    return pltpu.CompilerParams(vmem_limit_bytes=megabytes << 20)


def cost(us):
    return pl.CostEstimate(flops=int(us * 1e9), bytes_accessed=int(us * 3e6), transcendentals=0)


def run_legendre(wave, lev, levels, wave_table, factor, spectra, legendre):
    pairs, lat, slots = legendre.shape
    return pl.pallas_call(
        functools.partial(legendre_kernel, wave, lev, pairs),
        in_specs=[SMEM, SMEM, HBM, HBM],
        out_specs=[VMEM, VMEM],
        out_shape=[jax.ShapeDtypeStruct((2, 8 * pairs, 128), F32),
                   jax.ShapeDtypeStruct((levels, 24, 128), F32)],
        scratch_shapes=[pltpu.VMEM(spectra.shape, F32), pltpu.VMEM((pairs, 8, slots), F32),
                        pltpu.VMEM(legendre.shape, F32), pltpu.VMEM((24, 128), F32),
                        pltpu.SemaphoreType.DMA((pairs + 1,))],
        compiler_params=params(), cost_estimate=cost(3.0), name="legendre_inverse",
    )(wave_table, factor, spectra, legendre)


def run_gather(pairs, lat_owner, ft, recv):
    return pl.pallas_call(
        functools.partial(gather_kernel, pairs),
        in_specs=[SMEM, VMEM, VMEM],
        out_specs=VMEM,
        out_shape=jax.ShapeDtypeStruct((lat_owner.shape[0], 2, 128), F32),
        scratch_shapes=[pltpu.VMEM((24, 128), F32), pltpu.VMEM((2, 128, 128), F32),
                        pltpu.VMEM((2, 128, 128), F32)],
        compiler_params=params(), cost_estimate=cost(1.0), name="add_geopotential",
    )(lat_owner, ft, recv)


def run_tables(wave, lat_owner, row_points):
    return pl.pallas_call(
        functools.partial(table_kernel, wave),
        in_specs=[SMEM, SMEM],
        out_specs=[VMEM] * 4,
        out_shape=[jax.ShapeDtypeStruct((2 * COARSE, QUARTER), BF16)] * 2
        + [jax.ShapeDtypeStruct((FINE, QUARTER), F32)] * 2,
        compiler_params=params(), cost_estimate=cost(2.0), name="angle_tables",
    )(lat_owner, row_points)


def run_grid(wave, lat_owner, row_points, weights, order, recv, tables):
    return pl.pallas_call(
        functools.partial(grid_kernel, wave),
        in_specs=[SMEM, SMEM, SMEM] + [VMEM] * 6,
        out_specs=[VMEM, VMEM],
        out_shape=[jax.ShapeDtypeStruct(recv.shape, F32),
                   jax.ShapeDtypeStruct((4, 8, QUARTER), F32)],
        compiler_params=params(), cost_estimate=cost(5.0), name="grid_space",
    )(lat_owner, row_points, weights, order, recv, *tables)


def run_layout(wave, lat_owner, row_points, terms):
    return pl.pallas_call(
        functools.partial(layout_kernel, wave),
        in_specs=[SMEM, SMEM, VMEM],
        out_specs=VMEM,
        out_shape=jax.ShapeDtypeStruct((1, 1, 3, PMAX), F32),
        scratch_shapes=[pltpu.VMEM((8, 5504), F32)],
        compiler_params=params(), cost_estimate=cost(2.0), name="grid_terms",
    )(lat_owner, row_points, terms)


def run_direct(wave, wave_table, lat_owner, recv, legendre):
    pairs, lat, slots = legendre.shape
    return pl.pallas_call(
        functools.partial(direct_kernel, wave, pairs),
        in_specs=[SMEM, SMEM, VMEM, HBM],
        out_specs=VMEM,
        out_shape=jax.ShapeDtypeStruct((pairs, 1, 3, 2, slots), F32),
        scratch_shapes=[pltpu.VMEM((2, 64, 128), F32), pltpu.VMEM(legendre.shape, F32),
                        pltpu.SemaphoreType.DMA((pairs,))],
        compiler_params=params(), cost_estimate=cost(3.0), name="legendre_direct",
    )(wave_table, lat_owner, recv, legendre)


def spectral_order(wave_table, waves):
    return jnp.transpose(wave_table.reshape(waves, -1)).reshape(1, -1)


def per_device(spectra, legendre, wave_table, lat_owner, row_points, weights, layer_depth_factor):
    waves, levels = lax.axis_size("wave"), lax.axis_size("lev")
    wave = functools.partial(lax.axis_index, "wave")
    lev = functools.partial(lax.axis_index, "lev")
    pairs = spectra.shape[0]
    ft, thick = run_legendre(wave, lev, levels, wave_table, layer_depth_factor, spectra, legendre)
    arrived = lax.all_to_all(thick, "lev", split_axis=0, concat_axis=0, tiled=True)
    tables = run_tables(wave, lat_owner, row_points)
    outgoing = run_gather(pairs, lat_owner, ft, arrived)
    arrived = lax.all_to_all(outgoing, "wave", split_axis=0, concat_axis=0, tiled=True)
    order = spectral_order(wave_table, waves)
    outgoing, terms = run_grid(wave, lat_owner, row_points, weights, order, arrived, tables)
    arrived = lax.all_to_all(outgoing, "wave", split_axis=0, concat_axis=0, tiled=True)
    grid_terms = run_layout(wave, lat_owner, row_points, terms)
    return run_direct(wave, wave_table, lat_owner, arrived, legendre), grid_terms


def solution(mesh):
    placed = (
        P("wave", "lev", None, None, None),
        P("wave", None, None),
        P(),
        P(),
        P(),
        P(),
        P("lev"),
    )
    return jax.shard_map(
        per_device,
        mesh=mesh,
        in_specs=placed,
        out_specs=(P("wave", "lev", None, None, None), P("wave", "lev", None, None)),
        check_vma=False,
    )
```

```python
import functools

import jax
import jax.numpy as jnp
from jax import lax
from jax.experimental import pallas as pl
from jax.experimental.pallas import tpu as pltpu
from jax.sharding import PartitionSpec as P

PMAX = 5136
QUARTER = 1408
COARSE = 80
FINE = 16
F32 = jnp.float32
BF16 = jnp.bfloat16
NN = (((1,), (0,)), ((), ()))
NT = (((1,), (1,)), ((), ()))

COS_POLY = (1.0, -19.73920440673828, 64.93911743164062, -85.45014190673828,
            60.16762924194336, -25.967599868774414, 6.528658390045166)
SIN_POLY = (6.2831854820251465, -41.34170150756836, 81.60513305664062, -76.70301818847656,
            42.02592849731445, -14.899847030639648, 3.2381374835968018)

SMEM = pl.BlockSpec(memory_space=pltpu.SMEM)
VMEM = pl.BlockSpec(memory_space=pltpu.VMEM)
HBM = pl.BlockSpec(memory_space=pl.ANY)


def split(x):
    hi = x.astype(BF16)
    return hi, (x - hi.astype(F32)).astype(BF16)


def dot(a, b, dims=NN):
    return lax.dot_general(a, b, dims, preferred_element_type=F32)


def iota(shape, axis):
    return lax.broadcasted_iota(jnp.int32, shape, axis)


def own_entry(owner_ref, table_ref, me, start):
    total = start
    for j in range(owner_ref.shape[0]):
        total = total + jnp.where(owner_ref[j] == me, table_ref[j], jnp.zeros_like(start))
    return total


SOURCE_ROWS = ((0, 4), (1, 0), (2, 2), (4, 5), (5, 1), (6, 3))


def legendre_kernel(wave, lev, pairs, group, wt_ref, factor_ref, spectra_ref, legendre_ref,
                    ft_ref, send_ref, xs_ref, xx_ref, lg_ref, t_ref, sem):
    me, level = wave(), lev()
    copies = [pltpu.make_async_copy(spectra_ref, xs_ref, sem.at[0])]
    for p in range(pairs):
        copies.append(pltpu.make_async_copy(legendre_ref.at[p], lg_ref.at[p], sem.at[1 + p]))
    for copy in copies:
        copy.start()
    ft_ref[...] = jnp.zeros_like(ft_ref)
    xx_ref[...] = jnp.zeros_like(xx_ref)
    t_ref[...] = jnp.zeros_like(t_ref)
    copies[0].wait()
    for p in range(pairs):
        for f in range(3):
            xx_ref[p, 2 * f:2 * f + 2, :] = xs_ref[p, 0, f, :, :]
    lane = iota((1, 128), 1)
    for first in range(0, pairs, group):
        members = range(first, min(first + group, pairs))
        for p in members:
            copies[1 + p].wait()
        sums = []
        for p in members:
            bound = 1280 - wt_ref[me * pairs + p]
            x = xx_ref[p]
            low = iota(x.shape, 1) < bound
            s = jnp.concatenate([jnp.where(low, x, 0.0), jnp.where(low, 0.0, x)], axis=0)
            lhs = jnp.concatenate(split(s), axis=0)
            rhs = jnp.concatenate(split(lg_ref[p]), axis=0)
            o = dot(lhs, rhs, NT)
            f = o[:16] + o[16:]
            sums.append(f + pltpu.roll(f, 64, 1))
        for p, f in zip(members, sums):
            for half in range(2):
                for to, source in SOURCE_ROWS:
                    ft_ref[half, 8 * p + to:8 * p + to + 1, :] = f[8 * half + source:8 * half + source + 1]
                t_ref[pairs * half + p:pairs * half + p + 1, :] = jnp.where(
                    lane < 64, f[8 * half + 4:8 * half + 5], f[8 * half + 5:8 * half + 6])
    thick = t_ref[...] * factor_ref[0]
    for k in range(send_ref.shape[0]):
        send_ref[k] = thick * jnp.where(k <= level, 1.0, 0.0).astype(F32)


def gather_kernel(pairs, owner_ref, ft_ref, recv_ref, send_ref, g_ref, f_ref, v_ref):
    g_ref[...] = jnp.sum(recv_ref[...], axis=0)
    for half in range(2):
        f_ref[half, 0:8 * pairs, :] = ft_ref[half]
        f_ref[half, 8 * pairs:, :] = jnp.zeros((128 - 8 * pairs, 128), F32)
        for p in range(pairs):
            row = g_ref[pairs * half + p:pairs * half + p + 1, :]
            f_ref[half, 8 * p + 3:8 * p + 4, :] = row
            f_ref[half, 8 * p + 7:8 * p + 8, :] = pltpu.roll(row, 64, 1)
        v_ref[half] = jnp.transpose(f_ref[half])
    for j in range(owner_ref.shape[0]):
        to = owner_ref[j]
        for half in range(2):
            send_ref[to, half:half + 1, :] = v_ref[half, j:j + 1, :]


def table_kernel(wave, owner_ref, points_ref, hi_ref, lo_ref, cos_ref, sin_ref):
    length = own_entry(owner_ref, points_ref, wave(), jnp.int32(0)).astype(F32)
    inverse = 1.0 / jnp.full((1, QUARTER), length, F32)
    point = iota((16, QUARTER), 1).astype(F32)
    row = iota((16, QUARTER), 0).astype(F32)

    def turn(wave_number):
        x = wave_number * point
        t = (x - jnp.floor(x * inverse + 0.5) * length) * inverse
        y = t * t
        c = jnp.full_like(y, COS_POLY[-1])
        s = jnp.full_like(y, SIN_POLY[-1])
        for a, b in zip(COS_POLY[-2::-1], SIN_POLY[-2::-1]):
            c = c * y + a
            s = s * y + b
        return c, s * t

    for i in range(COARSE // 16):
        c, s = turn((row + 16.0 * i) * FINE)
        at = pl.ds(16 * i, 16)
        hi_ref[at, :], lo_ref[at, :] = split(c)
        at = pl.ds(COARSE + 16 * i, 16)
        hi_ref[at, :], lo_ref[at, :] = split(s)
    c, s = turn(row)
    cos_ref[...] = c
    sin_ref[...] = s


def grid_kernel(wave, owner_ref, points_ref, weights_ref, order_ref, recv_ref, hi_ref, lo_ref,
                cos_ref, sin_ref, send_ref, terms_ref):
    me = wave()
    length = own_entry(owner_ref, points_ref, me, jnp.int32(0))
    weight = own_entry(owner_ref, weights_ref, me, jnp.float32(0))
    quarter = length // 4
    order = order_ref[...]
    fine = order & 15
    coarse = order >> 4
    a_row = iota((128, order.shape[1]), 0)
    pick = jnp.concatenate([
        jnp.where(coarse == a_row, 1.0, 0.0).astype(BF16),
        jnp.where(COARSE - 1 - coarse == a_row, 1.0, 0.0).astype(BF16)], axis=1)

    tops, lows = [], []
    for half in range(2):
        x = recv_ref[:, half, :]
        z = jnp.transpose(jnp.concatenate([x, pltpu.roll(x, 120, 1)], axis=0))
        xl = jnp.concatenate([z[16 * i:16 * i + 8] for i in range(5)], axis=1)
        hi = xl.astype(BF16).astype(F32)
        lo = xl - hi
        b_of = fine if half == 0 else FINE - 1 - fine
        tops.append(jnp.concatenate([jnp.where(b_of == b, hi, 0.0) for b in range(FINE)], axis=0).astype(BF16))
        lows.append(jnp.concatenate([jnp.where(b_of == b, lo, 0.0) for b in range(FINE)], axis=0).astype(BF16))
    lhs = jnp.concatenate([jnp.concatenate(tops, axis=1), jnp.concatenate(lows, axis=1)], axis=0)
    y = dot(lhs, pick, NT)
    y = y[:128] + y[128:]
    first = (iota((128, 128), 0) < 8) & (iota((128, 128), 1) == 0)
    y = y * jnp.where(first, 1.0, 2.0)
    in_real = (iota((128, 128), 0) & 7) < 4

    def swap(v):
        return pltpu.roll(v.reshape(FINE, 8, 128), 4, 1).reshape(128, 128)

    swapped = swap(y)
    lhs = jnp.concatenate([y, jnp.where(in_real, -swapped, swapped)], axis=1)
    lhs_hi, lhs_lo = split(lhs)
    lhs_both = jnp.concatenate([lhs_hi, lhs_lo], axis=0)

    acc = jnp.zeros((128, 256), F32)
    for start in range(0, QUARTER, 256):
        n = min(256, QUARTER - start)
        cols = slice(start, start + n)
        gap = jnp.zeros((48, n), BF16)
        t_hi = jnp.concatenate([hi_ref[0:80, cols], gap, hi_ref[80:160, cols], gap], axis=0)
        t_lo = jnp.concatenate([lo_ref[0:80, cols], gap, lo_ref[80:160, cols], gap], axis=0)
        part = dot(lhs_both, t_hi)
        part = part[:128] + part[128:] + dot(lhs_hi, t_lo)
        top = iota((8, n), 0) < 4
        turn_re, turn_im = [], []
        sums = {}

        def add(key, value):
            sums[key] = sums[key] + value if key in sums else value

        for b in range(FINE):
            c = jnp.broadcast_to(cos_ref[b:b + 1, cols], (8, n))
            s = jnp.broadcast_to(sin_ref[b:b + 1, cols], (8, n))
            turn_re.append(jnp.where(top, c, -s))
            turn_im.append(jnp.where(top, s, c) if b % 2 else None)
            rows = part[8 * b:8 * b + 8]
            add(("re", b % 4), rows * turn_re[b])
            if b % 2:
                add(("im", b % 4), rows * turn_im[b])

        def fold(v):
            return v + pltpu.roll(v, 4, 0)

        even_sum = fold(sums["re", 0] + sums["re", 2])
        even_dif = fold(sums["re", 0] - sums["re", 2])
        odd_sum = fold(sums["re", 1] + sums["re", 3])
        odd_dif = fold(sums["im", 3] - sums["im", 1])
        inside = iota((8, n), 1) + start < quarter
        kind = iota((8, n), 0) & 3
        terms = []
        for r, field in enumerate((even_sum + odd_sum, even_dif + odd_dif,
                                   even_sum - odd_sum, even_dif - odd_dif)):
            square = field * field
            energy = 0.5 * (pltpu.roll(square, 7, 0) + pltpu.roll(square, 6, 0)) + pltpu.roll(field, 5, 0)
            flux = field * field[0:1]
            value = jnp.where(kind == 0, energy, jnp.where(kind == 3, 0.0, flux))
            value = jnp.where(inside, value, 0.0)
            terms_ref[r, :, cols] = value
            terms.append(value)
        even, odd = terms[0] + terms[2], terms[1] + terms[3]
        real, imag = terms[0] - terms[2], terms[1] - terms[3]
        folded = {0: even + odd, 2: even - odd}
        back = []
        for b in range(FINE):
            if b % 2 == 0:
                back.append(folded[b % 4] * turn_re[b])
            elif b % 4 == 1:
                back.append(real * turn_re[b] - imag * turn_im[b])
            else:
                back.append(real * turn_re[b] + imag * turn_im[b])
        g_hi, g_lo = split(jnp.concatenate(back, axis=0))
        both = dot(jnp.concatenate([g_hi, g_lo], axis=0), t_hi, NT)
        acc = acc + both[:128] + both[128:] + dot(g_hi, t_lo, NT)

    swapped = swap(acc[:, 128:])
    analysed = acc[:, :128] + jnp.where(in_real, swapped, -swapped)
    analysed = analysed * (weight / jnp.full((1, 128), length.astype(F32), F32))

    a_hi, a_lo = split(analysed)
    v = dot(jnp.concatenate([a_hi, a_lo], axis=1), jnp.concatenate([pick, pick], axis=0))
    for half in range(2):
        b_of = fine if half == 0 else FINE - 1 - fine
        cols = slice(order.shape[1] * half, order.shape[1] * (half + 1))
        xl = jnp.zeros((8, order.shape[1]), F32)
        for b in range(FINE):
            xl = xl + jnp.where(b_of == b, v[8 * b:8 * b + 8, cols], 0.0)
        pieces = []
        for i in range(5):
            pieces += [xl[:, 128 * i:128 * i + 128], jnp.zeros((8, 128), F32)]
        z = jnp.transpose(jnp.concatenate(pieces + [jnp.zeros((48, 128), F32)], axis=0))
        send_ref[:, half, :] = z[:64] + pltpu.roll(z[64:], 8, 1)


def layout_kernel(wave, owner_ref, points_ref, terms_ref, out_ref, line_ref):
    quarter = own_entry(owner_ref, points_ref, wave(), jnp.int32(0)) // 4
    line_ref[...] = jnp.zeros_like(line_ref)
    gap = jnp.zeros((8, 128), F32)
    for r in range(4):
        at = r * quarter
        value = jnp.concatenate([terms_ref[r], gap], axis=1)
        value = pltpu.roll(value, at % 128, 1)
        where = pl.ds(pl.multiple_of(at // 128 * 128, 128), QUARTER + 128)
        line_ref[:, where] = line_ref[:, where] + value
    for f in range(3):
        out_ref[0, f, 0:1, :] = line_ref[f:f + 1, 0:PMAX]


def parts_kernel(legendre_ref, after_ref, parts_ref):
    for p in range(parts_ref.shape[0]):
        parts_ref[p] = jnp.concatenate(split(legendre_ref[p]), axis=0)


def direct_kernel(wave, pairs, wt_ref, owner_ref, recv_ref, parts_ref, legendre_ref, out_ref,
                  v_ref, lg_ref, sem):
    me = wave()
    held = parts_ref.shape[0]
    copy = pltpu.make_async_copy(legendre_ref.at[pl.ds(held, pairs - held)], lg_ref, sem)
    copy.start()
    for j in range(owner_ref.shape[0]):
        source = owner_ref[j]
        for half in range(2):
            v_ref[half, j:j + 1, :] = recv_ref[source, half:half + 1, :]
    lane = iota((16, 128), 1)
    turned = [jnp.transpose(jnp.concatenate([v_ref[half], v_ref[half]], axis=0)) for half in range(2)]

    def one(p, rhs):
        bound = 1280 - wt_ref[me * pairs + p]
        q = jnp.concatenate([t[8 * p:8 * p + 8] for t in turned], axis=0)
        hi, lo = split(q)
        lhs = jnp.concatenate([hi, jnp.where(lane < 64, lo, jnp.zeros_like(lo))], axis=0)
        o = dot(lhs, rhs)
        o = o[:16] + o[16:]
        y = jnp.where(iota((8, o.shape[1]), 1) < bound, o[:8], o[8:])
        for f in range(3):
            out_ref[p, 0, f, 0:1, :] = y[f:f + 1]
            out_ref[p, 0, f, 1:2, :] = y[4 + f:5 + f]

    for p in range(held):
        one(p, parts_ref[p])
    copy.wait()
    for p in range(held, pairs):
        one(p, jnp.concatenate(split(lg_ref[p - held]), axis=0))


def params(megabytes=24):
    return pltpu.CompilerParams(vmem_limit_bytes=megabytes << 20)


def cost(us):
    return pl.CostEstimate(flops=int(us * 1e9), bytes_accessed=int(us * 3e6), transcendentals=0)


def run_legendre(wave, lev, levels, wave_table, factor, spectra, legendre):
    pairs, lat, slots = legendre.shape
    return pl.pallas_call(
        functools.partial(legendre_kernel, wave, lev, pairs, 5),
        in_specs=[SMEM, SMEM, HBM, HBM],
        out_specs=[VMEM, VMEM],
        out_shape=[jax.ShapeDtypeStruct((2, 8 * pairs, 128), F32),
                   jax.ShapeDtypeStruct((levels, 24, 128), F32)],
        scratch_shapes=[pltpu.VMEM(spectra.shape, F32), pltpu.VMEM((pairs, 8, slots), F32),
                        pltpu.VMEM(legendre.shape, F32), pltpu.VMEM((24, 128), F32),
                        pltpu.SemaphoreType.DMA((pairs + 1,))],
        compiler_params=params(56), cost_estimate=cost(3.0), name="legendre_inverse",
    )(wave_table, factor, spectra, legendre)


def run_gather(pairs, lat_owner, ft, recv):
    return pl.pallas_call(
        functools.partial(gather_kernel, pairs),
        in_specs=[SMEM, VMEM, VMEM],
        out_specs=VMEM,
        out_shape=jax.ShapeDtypeStruct((lat_owner.shape[0], 2, 128), F32),
        scratch_shapes=[pltpu.VMEM((24, 128), F32), pltpu.VMEM((2, 128, 128), F32),
                        pltpu.VMEM((2, 128, 128), F32)],
        compiler_params=params(), cost_estimate=cost(1.0), name="add_geopotential",
    )(lat_owner, ft, recv)


def run_tables(wave, lat_owner, row_points):
    return pl.pallas_call(
        functools.partial(table_kernel, wave),
        in_specs=[SMEM, SMEM],
        out_specs=[VMEM] * 4,
        out_shape=[jax.ShapeDtypeStruct((2 * COARSE, QUARTER), BF16)] * 2
        + [jax.ShapeDtypeStruct((FINE, QUARTER), F32)] * 2,
        compiler_params=params(), cost_estimate=cost(2.0), name="angle_tables",
    )(lat_owner, row_points)


def run_grid(wave, lat_owner, row_points, weights, order, recv, tables):
    return pl.pallas_call(
        functools.partial(grid_kernel, wave),
        in_specs=[SMEM, SMEM, SMEM] + [VMEM] * 6,
        out_specs=[VMEM, VMEM],
        out_shape=[jax.ShapeDtypeStruct(recv.shape, F32),
                   jax.ShapeDtypeStruct((4, 8, QUARTER), F32)],
        compiler_params=params(), cost_estimate=cost(5.0), name="grid_space",
    )(lat_owner, row_points, weights, order, recv, *tables)


def run_layout(wave, lat_owner, row_points, terms):
    return pl.pallas_call(
        functools.partial(layout_kernel, wave),
        in_specs=[SMEM, SMEM, VMEM],
        out_specs=VMEM,
        out_shape=jax.ShapeDtypeStruct((1, 3, 1, PMAX), F32),
        scratch_shapes=[pltpu.VMEM((8, 5504), F32)],
        compiler_params=params(), cost_estimate=cost(2.0), name="grid_terms",
    )(lat_owner, row_points, terms)


def run_parts(legendre, after):
    pairs, lat, slots = legendre.shape
    held = pairs * 7 // 10
    return pl.pallas_call(
        parts_kernel, in_specs=[VMEM, HBM], out_specs=VMEM,
        out_shape=jax.ShapeDtypeStruct((held, 2 * lat, slots), BF16),
        compiler_params=params(), cost_estimate=cost(1.0), name="legendre_parts",
    )(legendre, after)


def run_direct(wave, wave_table, lat_owner, recv, parts, legendre):
    pairs, lat, slots = legendre.shape
    return pl.pallas_call(
        functools.partial(direct_kernel, wave, pairs),
        in_specs=[SMEM, SMEM, VMEM, VMEM, HBM],
        out_specs=VMEM,
        out_shape=jax.ShapeDtypeStruct((pairs, 1, 3, 2, slots), F32),
        scratch_shapes=[pltpu.VMEM((2, 64, 128), F32),
                        pltpu.VMEM((pairs - parts.shape[0], lat, slots), F32),
                        pltpu.SemaphoreType.DMA],
        compiler_params=params(49), cost_estimate=cost(3.0), name="legendre_direct",
    )(wave_table, lat_owner, recv, parts, legendre)


def spectral_order(wave_table, waves):
    return jnp.transpose(wave_table.reshape(waves, -1)).reshape(1, -1)


def per_device(spectra, legendre, wave_table, lat_owner, row_points, weights, layer_depth_factor):
    waves, levels = lax.axis_size("wave"), lax.axis_size("lev")
    wave = functools.partial(lax.axis_index, "wave")
    lev = functools.partial(lax.axis_index, "lev")
    pairs = spectra.shape[0]
    ft, thick = run_legendre(wave, lev, levels, wave_table, layer_depth_factor, spectra, legendre)
    arrived = lax.all_to_all(thick, "lev", split_axis=0, concat_axis=0, tiled=True)
    tables = run_tables(wave, lat_owner, row_points)
    outgoing = run_gather(pairs, lat_owner, ft, arrived)
    arrived = lax.all_to_all(outgoing, "wave", split_axis=0, concat_axis=0, tiled=True)
    order = spectral_order(wave_table, waves)
    outgoing, terms = run_grid(wave, lat_owner, row_points, weights, order, arrived, tables)
    arrived = lax.all_to_all(outgoing, "wave", split_axis=0, concat_axis=0, tiled=True)
    grid_terms = run_layout(wave, lat_owner, row_points, terms)
    parts = run_parts(legendre, terms)
    spectral_out = run_direct(wave, wave_table, lat_owner, arrived, parts, legendre)
    return spectral_out, jnp.transpose(grid_terms, (0, 2, 1, 3))


def solution(mesh):
    placed = (
        P("wave", "lev", None, None, None),
        P("wave", None, None),
        P(),
        P(),
        P(),
        P(),
        P("lev"),
    )
    return jax.shard_map(
        per_device,
        mesh=mesh,
        in_specs=placed,
        out_specs=(P("wave", "lev", None, None, None), P("wave", "lev", None, None)),
        check_vma=False,
    )
```

```python
import functools

import jax
import jax.numpy as jnp
from jax import lax
from jax.experimental import pallas as pl
from jax.experimental.pallas import tpu as pltpu
from jax.sharding import PartitionSpec as P

PMAX = 5136
QUARTER = 1408
COARSE = 80
FINE = 16
GROUPS = (5, 5)
F32 = jnp.float32
BF16 = jnp.bfloat16
NN = (((1,), (0,)), ((), ()))
NT = (((1,), (1,)), ((), ()))

COS_POLY = (1.0, -19.73920440673828, 64.93911743164062, -85.45014190673828,
            60.16762924194336, -25.967599868774414, 6.528658390045166)
SIN_POLY = (6.2831854820251465, -41.34170150756836, 81.60513305664062, -76.70301818847656,
            42.02592849731445, -14.899847030639648, 3.2381374835968018)

SMEM = pl.BlockSpec(memory_space=pltpu.SMEM)
VMEM = pl.BlockSpec(memory_space=pltpu.VMEM)
HBM = pl.BlockSpec(memory_space=pl.ANY)


def split(x):
    hi = x.astype(BF16)
    return hi, (x - hi.astype(F32)).astype(BF16)


def dot(a, b, dims=NN):
    return lax.dot_general(a, b, dims, preferred_element_type=F32)


def iota(shape, axis):
    return lax.broadcasted_iota(jnp.int32, shape, axis)


def own_entry(owner_ref, table_ref, me, start):
    total = start
    for j in range(owner_ref.shape[0]):
        total = total + jnp.where(owner_ref[j] == me, table_ref[j], jnp.zeros_like(start))
    return total


SOURCE_ROWS = ((0, 4), (1, 0), (2, 2), (4, 5), (5, 1), (6, 3))


def legendre_kernel(wave, lev, pairs, groups, wt_ref, factor_ref, spectra_ref, legendre_ref,
                    ft_ref, send_ref, xs_ref, xx_ref, lg_ref, t_ref, own_ref, sem):
    me, level = wave(), lev()
    copies = [pltpu.make_async_copy(spectra_ref, xs_ref, sem.at[0])]
    for p in range(pairs):
        copies.append(pltpu.make_async_copy(legendre_ref.at[p], lg_ref.at[p], sem.at[1 + p]))
    copies.append(pltpu.make_async_copy(factor_ref, own_ref, sem.at[1 + pairs]))
    for copy in copies:
        copy.start()
    ft_ref[...] = jnp.zeros_like(ft_ref)
    xx_ref[...] = jnp.zeros_like(xx_ref)
    t_ref[...] = jnp.zeros_like(t_ref)
    copies[0].wait()
    for p in range(pairs):
        for f in range(3):
            xx_ref[p, 2 * f:2 * f + 2, :] = xs_ref[p, 0, f, :, :]
    lane = iota((1, 128), 1)
    for at, size in enumerate(groups):
        members = range(sum(groups[:at]), min(sum(groups[:at]) + size, pairs))
        for p in members:
            copies[1 + p].wait()
        sums = []
        for p in members:
            bound = 1280 - wt_ref[me * pairs + p]
            x = xx_ref[p]
            low = iota(x.shape, 1) < bound
            s = jnp.concatenate([jnp.where(low, x, 0.0), jnp.where(low, 0.0, x)], axis=0)
            lhs = jnp.concatenate(split(s), axis=0)
            rhs = jnp.concatenate(split(lg_ref[p]), axis=0)
            o = dot(lhs, rhs, NT)
            f = o[:16] + o[16:]
            sums.append(f + pltpu.roll(f, 64, 1))
        for p, f in zip(members, sums):
            for half in range(2):
                for to, source in SOURCE_ROWS:
                    ft_ref[half, 8 * p + to:8 * p + to + 1, :] = f[8 * half + source:8 * half + source + 1]
                t_ref[pairs * half + p:pairs * half + p + 1, :] = jnp.where(
                    lane < 64, f[8 * half + 4:8 * half + 5], f[8 * half + 5:8 * half + 6])
    copies[1 + pairs].wait()
    thick = t_ref[...] * own_ref[...]
    for k in range(send_ref.shape[0]):
        send_ref[k] = thick * jnp.where(k <= level, 1.0, 0.0).astype(F32)


def arrange_kernel(owner_ref, ft_ref, base_ref, f_ref, v_ref):
    rows = ft_ref.shape[1]
    for half in range(2):
        f_ref[half, 0:rows, :] = ft_ref[half]
        f_ref[half, rows:, :] = jnp.zeros((128 - rows, 128), F32)
        v_ref[half] = jnp.transpose(f_ref[half])
    for j in range(owner_ref.shape[0]):
        to = owner_ref[j]
        for half in range(2):
            base_ref[half, pl.ds(to, 1), :] = v_ref[half, j:j + 1, :]


def gather_kernel(pairs, owner_ref, base_ref, recv_ref, send_ref, g_ref, f_ref, v_ref):
    g_ref[...] = jnp.sum(recv_ref[...], axis=0)
    f_ref[...] = jnp.zeros_like(f_ref)
    for half in range(2):
        for p in range(pairs):
            row = g_ref[pairs * half + p:pairs * half + p + 1, :]
            f_ref[half, 8 * p + 3:8 * p + 4, :] = row
            f_ref[half, 8 * p + 7:8 * p + 8, :] = pltpu.roll(row, 64, 1)
        v_ref[half] = jnp.transpose(f_ref[half])
    for j in range(owner_ref.shape[0]):
        to = owner_ref[j]
        for half in range(2):
            send_ref[to, half:half + 1, :] = v_ref[half, j:j + 1, :] + base_ref[half, pl.ds(to, 1), :]


def table_kernel(wave, owner_ref, points_ref, weights_ref, order_ref,
                 hi_ref, lo_ref, cos_ref, sin_ref, own_ref, pick_ref):
    me = wave()
    points = own_entry(owner_ref, points_ref, me, jnp.int32(0))
    length = points.astype(F32)
    weight = own_entry(owner_ref, weights_ref, me, jnp.float32(0))
    shape = (8, own_ref.shape[1])
    own_ref[...] = jnp.where(iota(shape, 0) == 0, jnp.full(shape, (points // 4).astype(F32), F32),
                             weight / jnp.full(shape, length, F32))
    coarse = order_ref[...] >> 4
    columns = coarse.shape[1]
    a_row = iota((128, columns), 0)
    pick_ref[:, :columns] = jnp.where(coarse == a_row, 1.0, 0.0).astype(BF16)
    pick_ref[:, columns:] = jnp.where(COARSE - 1 - coarse == a_row, 1.0, 0.0).astype(BF16)
    inverse = 1.0 / jnp.full((1, QUARTER), length, F32)
    point = iota((16, QUARTER), 1).astype(F32)
    row = iota((16, QUARTER), 0).astype(F32)

    def turn(wave_number):
        x = wave_number * point
        t = (x - jnp.floor(x * inverse + 0.5) * length) * inverse
        y = t * t
        c = jnp.full_like(y, COS_POLY[-1])
        s = jnp.full_like(y, SIN_POLY[-1])
        for a, b in zip(COS_POLY[-2::-1], SIN_POLY[-2::-1]):
            c = c * y + a
            s = s * y + b
        return c, s * t

    for i in range(COARSE // 16):
        c, s = turn((row + 16.0 * i) * FINE)
        at = pl.ds(16 * i, 16)
        hi_ref[at, :], lo_ref[at, :] = split(c)
        at = pl.ds(COARSE + 16 * i, 16)
        hi_ref[at, :], lo_ref[at, :] = split(s)
    c, s = turn(row)
    cos_ref[...] = c
    sin_ref[...] = s


def grid_kernel(order_ref, recv_ref, hi_ref, lo_ref, cos_ref, sin_ref, own_ref, pick_ref,
                send_ref, terms_ref):
    order = order_ref[...]
    fine = order & 15
    pick = pick_ref[...]

    tops, lows = [], []
    for half in range(2):
        x = recv_ref[:, half, :]
        z = jnp.transpose(jnp.concatenate([x, pltpu.roll(x, 120, 1)], axis=0))
        xl = jnp.concatenate([z[16 * i:16 * i + 8] for i in range(5)], axis=1)
        hi = xl.astype(BF16).astype(F32)
        lo = xl - hi
        b_of = fine if half == 0 else FINE - 1 - fine
        tops.append(jnp.concatenate([jnp.where(b_of == b, hi, 0.0) for b in range(FINE)], axis=0).astype(BF16))
        lows.append(jnp.concatenate([jnp.where(b_of == b, lo, 0.0) for b in range(FINE)], axis=0).astype(BF16))
    lhs = jnp.concatenate([jnp.concatenate(tops, axis=1), jnp.concatenate(lows, axis=1)], axis=0)
    y = dot(lhs, pick, NT)
    y = y[:128] + y[128:]
    first = (iota((128, 128), 0) < 8) & (iota((128, 128), 1) == 0)
    y = y * jnp.where(first, 1.0, 2.0)
    in_real = (iota((128, 128), 0) & 7) < 4

    def swap(v):
        return pltpu.roll(v.reshape(FINE, 8, 128), 4, 1).reshape(128, 128)

    swapped = swap(y)
    lhs = jnp.concatenate([y, jnp.where(in_real, -swapped, swapped)], axis=1)
    lhs_hi, lhs_lo = split(lhs)
    lhs_both = jnp.concatenate([lhs_hi, lhs_lo], axis=0)

    acc = jnp.zeros((128, 256), F32)
    for start in range(0, QUARTER, 256):
        n = min(256, QUARTER - start)
        cols = slice(start, start + n)
        gap = jnp.zeros((48, n), BF16)
        t_hi = jnp.concatenate([hi_ref[0:80, cols], gap, hi_ref[80:160, cols], gap], axis=0)
        t_lo = jnp.concatenate([lo_ref[0:80, cols], gap, lo_ref[80:160, cols], gap], axis=0)
        part = dot(lhs_both, t_hi)
        part = part[:128] + part[128:] + dot(lhs_hi, t_lo)
        top = iota((8, n), 0) < 4
        turn_re, turn_im = [], []
        sums = {}

        def add(key, value):
            sums[key] = sums[key] + value if key in sums else value

        for b in range(FINE):
            c = jnp.broadcast_to(cos_ref[b:b + 1, cols], (8, n))
            s = jnp.broadcast_to(sin_ref[b:b + 1, cols], (8, n))
            turn_re.append(jnp.where(top, c, -s))
            turn_im.append(jnp.where(top, s, c) if b % 2 else None)
            rows = part[8 * b:8 * b + 8]
            add(("re", b % 4), rows * turn_re[b])
            if b % 2:
                add(("im", b % 4), rows * turn_im[b])

        def fold(v):
            return v + pltpu.roll(v, 4, 0)

        even_sum = fold(sums["re", 0] + sums["re", 2])
        even_dif = fold(sums["re", 0] - sums["re", 2])
        odd_sum = fold(sums["re", 1] + sums["re", 3])
        odd_dif = fold(sums["im", 3] - sums["im", 1])
        inside = (iota((8, n), 1) + start).astype(F32) < own_ref[0:1, 0:n]
        kind = iota((8, n), 0) & 3
        terms = []
        for r, field in enumerate((even_sum + odd_sum, even_dif + odd_dif,
                                   even_sum - odd_sum, even_dif - odd_dif)):
            square = field * field
            energy = 0.5 * (pltpu.roll(square, 7, 0) + pltpu.roll(square, 6, 0)) + pltpu.roll(field, 5, 0)
            flux = field * field[0:1]
            value = jnp.where(kind == 0, energy, jnp.where(kind == 3, 0.0, flux))
            value = jnp.where(inside, value, 0.0)
            terms_ref[r, :, cols] = value
            terms.append(value)
        even, odd = terms[0] + terms[2], terms[1] + terms[3]
        real, imag = terms[0] - terms[2], terms[1] - terms[3]
        folded = {0: even + odd, 2: even - odd}
        back = []
        for b in range(FINE):
            if b % 2 == 0:
                back.append(folded[b % 4] * turn_re[b])
            elif b % 4 == 1:
                back.append(real * turn_re[b] - imag * turn_im[b])
            else:
                back.append(real * turn_re[b] + imag * turn_im[b])
        g_hi, g_lo = split(jnp.concatenate(back, axis=0))
        both = dot(jnp.concatenate([g_hi, g_lo], axis=0), t_hi, NT)
        acc = acc + both[:128] + both[128:] + dot(g_hi, t_lo, NT)

    swapped = swap(acc[:, 128:])
    analysed = acc[:, :128] + jnp.where(in_real, swapped, -swapped)
    analysed = analysed * own_ref[1:2, 0:128]

    a_hi, a_lo = split(analysed)
    v = dot(jnp.concatenate([a_hi, a_lo], axis=1), jnp.concatenate([pick, pick], axis=0))
    for half in range(2):
        b_of = fine if half == 0 else FINE - 1 - fine
        cols = slice(order.shape[1] * half, order.shape[1] * (half + 1))
        xl = jnp.zeros((8, order.shape[1]), F32)
        for b in range(FINE):
            xl = xl + jnp.where(b_of == b, v[8 * b:8 * b + 8, cols], 0.0)
        pieces = []
        for i in range(5):
            pieces += [xl[:, 128 * i:128 * i + 128], jnp.zeros((8, 128), F32)]
        z = jnp.transpose(jnp.concatenate(pieces + [jnp.zeros((48, 128), F32)], axis=0))
        send_ref[:, half, :] = z[:64] + pltpu.roll(z[64:], 8, 1)


def layout_kernel(wave, owner_ref, points_ref, terms_ref, out_ref, line_ref):
    quarter = own_entry(owner_ref, points_ref, wave(), jnp.int32(0)) // 4
    line_ref[...] = jnp.zeros_like(line_ref)
    gap = jnp.zeros((8, 128), F32)
    for r in range(4):
        at = r * quarter
        value = jnp.concatenate([terms_ref[r], gap], axis=1)
        value = pltpu.roll(value, at % 128, 1)
        where = pl.ds(pl.multiple_of(at // 128 * 128, 128), QUARTER + 128)
        line_ref[:, where] = line_ref[:, where] + value
    for f in range(3):
        out_ref[0, f, 0:1, :] = line_ref[f:f + 1, 0:PMAX]


def parts_kernel(legendre_ref, after_ref, parts_ref):
    for p in range(parts_ref.shape[0]):
        parts_ref[p] = jnp.concatenate(split(legendre_ref[p]), axis=0)


def direct_kernel(wave, pairs, wt_ref, owner_ref, recv_ref, parts_ref, legendre_ref, out_ref,
                  v_ref, lg_ref, y_ref, sem, out_sem):
    me = wave()
    held = parts_ref.shape[0]
    copy = pltpu.make_async_copy(legendre_ref.at[pl.ds(held, pairs - held)], lg_ref, sem)
    copy.start()
    for j in range(owner_ref.shape[0]):
        source = owner_ref[j]
        for half in range(2):
            v_ref[half, j:j + 1, :] = recv_ref[source, half:half + 1, :]
    lane = iota((16, 128), 1)
    turned = [jnp.transpose(jnp.concatenate([v_ref[half], v_ref[half]], axis=0)) for half in range(2)]

    def one(p, rhs):
        bound = 1280 - wt_ref[me * pairs + p]
        q = jnp.concatenate([t[8 * p:8 * p + 8] for t in turned], axis=0)
        hi, lo = split(q)
        lhs = jnp.concatenate([hi, jnp.where(lane < 64, lo, jnp.zeros_like(lo))], axis=0)
        o = dot(lhs, rhs)
        o = o[:16] + o[16:]
        y = jnp.where(iota((8, o.shape[1]), 1) < bound, o[:8], o[8:])
        for f in range(3):
            y_ref[p, 0, f, 0:1, :] = y[f:f + 1]
            y_ref[p, 0, f, 1:2, :] = y[4 + f:5 + f]

    def leave(first, last, slot):
        at = pl.ds(first, last - first)
        out = pltpu.make_async_copy(y_ref.at[at], out_ref.at[at], out_sem.at[slot])
        out.start()
        return out

    for p in range(held):
        one(p, parts_ref[p])
    outs = [leave(0, held, 0)]
    copy.wait()
    for p in range(held, pairs):
        one(p, jnp.concatenate(split(lg_ref[p - held]), axis=0))
    outs.append(leave(held, pairs, 1))
    for out in outs:
        out.wait()


def params(megabytes=24):
    return pltpu.CompilerParams(vmem_limit_bytes=megabytes << 20)


def cost(us):
    return pl.CostEstimate(flops=int(us * 1e9), bytes_accessed=int(us * 3e6), transcendentals=0)


def run_legendre(wave, lev, levels, wave_table, factor, spectra, legendre):
    pairs, lat, slots = legendre.shape
    return pl.pallas_call(
        functools.partial(legendre_kernel, wave, lev, pairs, GROUPS),
        in_specs=[SMEM, HBM, HBM, HBM],
        out_specs=[VMEM, VMEM],
        out_shape=[jax.ShapeDtypeStruct((2, 8 * pairs, 128), F32),
                   jax.ShapeDtypeStruct((levels, 24, 128), F32)],
        scratch_shapes=[pltpu.VMEM(spectra.shape, F32), pltpu.VMEM((pairs, 8, slots), F32),
                        pltpu.VMEM(legendre.shape, F32), pltpu.VMEM((24, 128), F32),
                        pltpu.VMEM((1, 1), F32), pltpu.SemaphoreType.DMA((pairs + 2,))],
        compiler_params=params(56), cost_estimate=cost(3.0), name="legendre_inverse",
    )(wave_table, factor.reshape(1, 1), spectra, legendre)


def run_arrange(lat_owner, ft):
    return pl.pallas_call(
        arrange_kernel,
        in_specs=[SMEM, VMEM],
        out_specs=VMEM,
        out_shape=jax.ShapeDtypeStruct((2, lat_owner.shape[0], 128), F32),
        scratch_shapes=[pltpu.VMEM((2, 128, 128), F32), pltpu.VMEM((2, 128, 128), F32)],
        compiler_params=params(), cost_estimate=cost(1.0), name="arrange_rows",
    )(lat_owner, ft)


def run_gather(pairs, lat_owner, base, recv):
    return pl.pallas_call(
        functools.partial(gather_kernel, pairs),
        in_specs=[SMEM, VMEM, VMEM],
        out_specs=VMEM,
        out_shape=jax.ShapeDtypeStruct((lat_owner.shape[0], 2, 128), F32),
        scratch_shapes=[pltpu.VMEM((24, 128), F32), pltpu.VMEM((2, 128, 128), F32),
                        pltpu.VMEM((2, 128, 128), F32)],
        compiler_params=params(), cost_estimate=cost(1.0), name="add_geopotential",
    )(lat_owner, base, recv)


def run_tables(wave, lat_owner, row_points, weights, order):
    return pl.pallas_call(
        functools.partial(table_kernel, wave),
        in_specs=[SMEM, SMEM, SMEM, VMEM],
        out_specs=[VMEM] * 6,
        out_shape=[jax.ShapeDtypeStruct((2 * COARSE, QUARTER), BF16)] * 2
        + [jax.ShapeDtypeStruct((FINE, QUARTER), F32)] * 2
        + [jax.ShapeDtypeStruct((8, 256), F32),
           jax.ShapeDtypeStruct((128, 2 * order.shape[1]), BF16)],
        compiler_params=params(), cost_estimate=cost(2.0), name="angle_tables",
    )(lat_owner, row_points, weights, order)


def run_grid(order, recv, tables):
    return pl.pallas_call(
        grid_kernel,
        in_specs=[VMEM] * 8,
        out_specs=[VMEM, VMEM],
        out_shape=[jax.ShapeDtypeStruct(recv.shape, F32),
                   jax.ShapeDtypeStruct((4, 8, QUARTER), F32)],
        compiler_params=params(), cost_estimate=cost(5.0), name="grid_space",
    )(order, recv, *tables)


def run_layout(wave, lat_owner, row_points, terms):
    return pl.pallas_call(
        functools.partial(layout_kernel, wave),
        in_specs=[SMEM, SMEM, VMEM],
        out_specs=VMEM,
        out_shape=jax.ShapeDtypeStruct((1, 3, 1, PMAX), F32),
        scratch_shapes=[pltpu.VMEM((8, 5504), F32)],
        compiler_params=params(), cost_estimate=cost(2.0), name="grid_terms",
    )(lat_owner, row_points, terms)


def run_parts(legendre, after):
    pairs, lat, slots = legendre.shape
    held = pairs * 9 // 10
    return pl.pallas_call(
        parts_kernel, in_specs=[VMEM, HBM], out_specs=VMEM,
        out_shape=jax.ShapeDtypeStruct((held, 2 * lat, slots), BF16),
        compiler_params=params(), cost_estimate=cost(1.0), name="legendre_parts",
    )(legendre, after)


def run_direct(wave, wave_table, lat_owner, recv, parts, legendre):
    pairs, lat, slots = legendre.shape
    return pl.pallas_call(
        functools.partial(direct_kernel, wave, pairs),
        in_specs=[SMEM, SMEM, VMEM, VMEM, HBM],
        out_specs=HBM,
        out_shape=jax.ShapeDtypeStruct((pairs, 1, 3, 2, slots), F32),
        scratch_shapes=[pltpu.VMEM((2, 64, 128), F32),
                        pltpu.VMEM((pairs - parts.shape[0], lat, slots), F32),
                        pltpu.VMEM((pairs, 1, 3, 2, slots), F32),
                        pltpu.SemaphoreType.DMA, pltpu.SemaphoreType.DMA((2,))],
        compiler_params=params(49), cost_estimate=cost(3.0), name="legendre_direct",
    )(wave_table, lat_owner, recv, parts, legendre)


def spectral_order(wave_table, waves):
    return jnp.transpose(wave_table.reshape(waves, -1)).reshape(1, -1)


def per_device(spectra, legendre, wave_table, lat_owner, row_points, weights, layer_depth_factor):
    waves, levels = lax.axis_size("wave"), lax.axis_size("lev")
    wave = functools.partial(lax.axis_index, "wave")
    lev = functools.partial(lax.axis_index, "lev")
    pairs = spectra.shape[0]
    ft, thick = run_legendre(wave, lev, levels, wave_table, layer_depth_factor, spectra, legendre)
    arrived = lax.all_to_all(thick, "lev", split_axis=0, concat_axis=0, tiled=True)
    order = spectral_order(wave_table, waves)
    tables = run_tables(wave, lat_owner, row_points, weights, order)
    outgoing = run_gather(pairs, lat_owner, run_arrange(lat_owner, ft), arrived)
    arrived = lax.all_to_all(outgoing, "wave", split_axis=0, concat_axis=0, tiled=True)
    outgoing, terms = run_grid(order, arrived, tables)
    arrived = lax.all_to_all(outgoing, "wave", split_axis=0, concat_axis=0, tiled=True)
    grid_terms = run_layout(wave, lat_owner, row_points, terms)
    parts = run_parts(legendre, terms)
    spectral_out = run_direct(wave, wave_table, lat_owner, arrived, parts, legendre)
    return spectral_out, jnp.transpose(grid_terms, (0, 2, 1, 3))


def solution(mesh):
    placed = (
        P("wave", "lev", None, None, None),
        P("wave", None, None),
        P(),
        P(),
        P(),
        P(),
        P("lev"),
    )
    return jax.shard_map(
        per_device,
        mesh=mesh,
        in_specs=placed,
        out_specs=(P("wave", "lev", None, None, None), P("wave", "lev", None, None)),
        check_vma=False,
    )
```

```python
import functools

import jax
import jax.numpy as jnp
from jax import lax
from jax.experimental import pallas as pl
from jax.experimental.pallas import tpu as pltpu
from jax.sharding import PartitionSpec as P

PMAX = 5136
QUARTER = 1408
COARSE = 80
FINE = 16
GROUPS = (5, 5)
F32 = jnp.float32
BF16 = jnp.bfloat16
NN = (((1,), (0,)), ((), ()))
NT = (((1,), (1,)), ((), ()))

COS_POLY = (1.0, -19.73920440673828, 64.93911743164062, -85.45014190673828,
            60.16762924194336, -25.967599868774414, 6.528658390045166)
SIN_POLY = (6.2831854820251465, -41.34170150756836, 81.60513305664062, -76.70301818847656,
            42.02592849731445, -14.899847030639648, 3.2381374835968018)

SMEM = pl.BlockSpec(memory_space=pltpu.SMEM)
VMEM = pl.BlockSpec(memory_space=pltpu.VMEM)
HBM = pl.BlockSpec(memory_space=pl.ANY)


def split(x):
    hi = x.astype(BF16)
    return hi, (x - hi.astype(F32)).astype(BF16)


def dot(a, b, dims=NN):
    return lax.dot_general(a, b, dims, preferred_element_type=F32)


def iota(shape, axis):
    return lax.broadcasted_iota(jnp.int32, shape, axis)


def own_entry(owner_ref, table_ref, me, start):
    total = start
    for j in range(owner_ref.shape[0]):
        total = total + jnp.where(owner_ref[j] == me, table_ref[j], jnp.zeros_like(start))
    return total


SOURCE_ROWS = ((0, 4), (1, 0), (2, 2), (4, 5), (5, 1), (6, 3))


def legendre_kernel(wave, lev, pairs, groups, wt_ref, factor_ref, spectra_ref, legendre_ref,
                    ft_ref, send_ref, xs_ref, xx_ref, lg_ref, t_ref, own_ref, table_ref, sem):
    me, level = wave(), lev()
    copies = [pltpu.make_async_copy(spectra_ref, xs_ref, sem.at[0])]
    for p in range(pairs):
        copies.append(pltpu.make_async_copy(legendre_ref.at[p], lg_ref.at[p], sem.at[1 + p]))
    copies.append(pltpu.make_async_copy(factor_ref, own_ref, sem.at[1 + pairs]))
    copies.append(pltpu.make_async_copy(wt_ref, table_ref, sem.at[2 + pairs]))
    for copy in copies:
        copy.start()
    ft_ref[...] = jnp.zeros_like(ft_ref)
    xx_ref[...] = jnp.zeros_like(xx_ref)
    copies[2 + pairs].wait()
    copies[0].wait()
    for p in range(pairs):
        for f in range(3):
            xx_ref[p, 2 * f:2 * f + 2, :] = xs_ref[p, 0, f, :, :]
    lane = iota((1, 128), 1)
    for at, size in enumerate(groups):
        members = range(sum(groups[:at]), min(sum(groups[:at]) + size, pairs))
        for p in members:
            copies[1 + p].wait()
        sums = []
        for p in members:
            bound = 1280 - table_ref[me * pairs + p]
            x = xx_ref[p]
            low = iota(x.shape, 1) < bound
            s = jnp.concatenate([jnp.where(low, x, 0.0), jnp.where(low, 0.0, x)], axis=0)
            lhs = jnp.concatenate(split(s), axis=0)
            rhs = jnp.concatenate(split(lg_ref[p]), axis=0)
            o = dot(lhs, rhs, NT)
            f = o[:16] + o[16:]
            sums.append(f + pltpu.roll(f, 64, 1))
        for p, f in zip(members, sums):
            for half in range(2):
                for to, source in SOURCE_ROWS:
                    ft_ref[half, 8 * p + to:8 * p + to + 1, :] = f[8 * half + source:8 * half + source + 1]
                t_ref[p, half:half + 1, :] = jnp.where(
                    lane < 64, f[8 * half + 4:8 * half + 5], f[8 * half + 5:8 * half + 6])
    copies[1 + pairs].wait()
    thick = t_ref[...] * own_ref[...]
    for k in range(send_ref.shape[0]):
        send_ref[k] = thick * jnp.where(k <= level, 1.0, 0.0).astype(F32)


def arrange_kernel(owner_ref, ft_ref, base_ref, f_ref, v_ref):
    rows = ft_ref.shape[1]
    for half in range(2):
        f_ref[half, 0:rows, :] = ft_ref[half]
        f_ref[half, rows:, :] = jnp.zeros((128 - rows, 128), F32)
        v_ref[half] = jnp.transpose(f_ref[half])
    for j in range(owner_ref.shape[0]):
        to = owner_ref[j]
        for half in range(2):
            base_ref[half, pl.ds(to, 1), :] = v_ref[half, j:j + 1, :]


def gather_kernel(pairs, owner_in_ref, base_ref, recv_ref, send_ref, g_ref, f_ref, v_ref, owner_ref, sem):
    copy = pltpu.make_async_copy(owner_in_ref, owner_ref, sem)
    copy.start()
    g_ref[...] = jnp.sum(recv_ref[...], axis=0)
    f_ref[...] = jnp.zeros_like(f_ref)
    for half in range(2):
        for p in range(pairs):
            row = g_ref[p, half:half + 1, :]
            f_ref[half, 8 * p + 3:8 * p + 4, :] = row
            f_ref[half, 8 * p + 7:8 * p + 8, :] = pltpu.roll(row, 64, 1)
        v_ref[half] = jnp.transpose(f_ref[half])
    copy.wait()
    for j in range(owner_ref.shape[0]):
        to = owner_ref[j]
        for half in range(2):
            send_ref[to, half:half + 1, :] = v_ref[half, j:j + 1, :] + base_ref[half, pl.ds(to, 1), :]


def table_kernel(wave, owner_ref, points_ref, weights_ref, order_ref,
                 hi_ref, lo_ref, cos_ref, sin_ref, own_ref, pick_ref):
    me = wave()
    points = own_entry(owner_ref, points_ref, me, jnp.int32(0))
    length = points.astype(F32)
    weight = own_entry(owner_ref, weights_ref, me, jnp.float32(0))
    shape = (8, own_ref.shape[1])
    own_ref[...] = jnp.where(iota(shape, 0) == 0, jnp.full(shape, (points // 4).astype(F32), F32),
                             weight / jnp.full(shape, length, F32))
    coarse = order_ref[...] >> 4
    columns = coarse.shape[1]
    a_row = iota((128, columns), 0)
    pick_ref[:, :columns] = jnp.where(coarse == a_row, 1.0, 0.0).astype(BF16)
    pick_ref[:, columns:] = jnp.where(COARSE - 1 - coarse == a_row, 1.0, 0.0).astype(BF16)
    inverse = 1.0 / jnp.full((1, QUARTER), length, F32)
    point = iota((16, QUARTER), 1).astype(F32)
    row = iota((16, QUARTER), 0).astype(F32)

    def turn(wave_number):
        x = wave_number * point
        t = (x - jnp.floor(x * inverse + 0.5) * length) * inverse
        y = t * t
        c = jnp.full_like(y, COS_POLY[-1])
        s = jnp.full_like(y, SIN_POLY[-1])
        for a, b in zip(COS_POLY[-2::-1], SIN_POLY[-2::-1]):
            c = c * y + a
            s = s * y + b
        return c, s * t

    for i in range(COARSE // 16):
        c, s = turn((row + 16.0 * i) * FINE)
        at = pl.ds(16 * i, 16)
        hi_ref[at, :], lo_ref[at, :] = split(c)
        at = pl.ds(COARSE + 16 * i, 16)
        hi_ref[at, :], lo_ref[at, :] = split(s)
    c, s = turn(row)
    cos_ref[...] = c
    sin_ref[...] = s


def grid_kernel(order_ref, recv_ref, hi_ref, lo_ref, cos_ref, sin_ref, own_ref, pick_ref,
                send_ref, terms_ref):
    order = order_ref[...]
    fine = order & 15
    pick = pick_ref[...]

    tops, lows = [], []
    for half in range(2):
        x = recv_ref[:, half, :]
        z = jnp.transpose(jnp.concatenate([x, pltpu.roll(x, 120, 1)], axis=0))
        xl = jnp.concatenate([z[16 * i:16 * i + 8] for i in range(5)], axis=1)
        hi = xl.astype(BF16).astype(F32)
        lo = xl - hi
        b_of = fine if half == 0 else FINE - 1 - fine
        tops.append(jnp.concatenate([jnp.where(b_of == b, hi, 0.0) for b in range(FINE)], axis=0).astype(BF16))
        lows.append(jnp.concatenate([jnp.where(b_of == b, lo, 0.0) for b in range(FINE)], axis=0).astype(BF16))
    lhs = jnp.concatenate([jnp.concatenate(tops, axis=1), jnp.concatenate(lows, axis=1)], axis=0)
    y = dot(lhs, pick, NT)
    y = y[:128] + y[128:]
    first = (iota((128, 128), 0) < 8) & (iota((128, 128), 1) == 0)
    y = y * jnp.where(first, 1.0, 2.0)
    in_real = (iota((128, 128), 0) & 7) < 4

    def swap(v):
        return pltpu.roll(v.reshape(FINE, 8, 128), 4, 1).reshape(128, 128)

    swapped = swap(y)
    lhs = jnp.concatenate([y, jnp.where(in_real, -swapped, swapped)], axis=1)
    lhs_hi, lhs_lo = split(lhs)
    lhs_both = jnp.concatenate([lhs_hi, lhs_lo], axis=0)

    acc = jnp.zeros((128, 256), F32)
    for start in range(0, QUARTER, 256):
        n = min(256, QUARTER - start)
        cols = slice(start, start + n)
        gap = jnp.zeros((48, n), BF16)
        t_hi = jnp.concatenate([hi_ref[0:80, cols], gap, hi_ref[80:160, cols], gap], axis=0)
        t_lo = jnp.concatenate([lo_ref[0:80, cols], gap, lo_ref[80:160, cols], gap], axis=0)
        part = dot(lhs_both, t_hi)
        part = part[:128] + part[128:] + dot(lhs_hi, t_lo)
        top = iota((8, n), 0) < 4
        turn_re, turn_im = [], []
        sums = {}

        def add(key, value):
            sums[key] = sums[key] + value if key in sums else value

        for b in range(FINE):
            c = jnp.broadcast_to(cos_ref[b:b + 1, cols], (8, n))
            s = jnp.broadcast_to(sin_ref[b:b + 1, cols], (8, n))
            turn_re.append(jnp.where(top, c, -s))
            turn_im.append(jnp.where(top, s, c) if b % 2 else None)
            rows = part[8 * b:8 * b + 8]
            add(("re", b % 4), rows * turn_re[b])
            if b % 2:
                add(("im", b % 4), rows * turn_im[b])

        def fold(v):
            return v + pltpu.roll(v, 4, 0)

        even_sum = fold(sums["re", 0] + sums["re", 2])
        even_dif = fold(sums["re", 0] - sums["re", 2])
        odd_sum = fold(sums["re", 1] + sums["re", 3])
        odd_dif = fold(sums["im", 3] - sums["im", 1])
        inside = (iota((8, n), 1) + start).astype(F32) < own_ref[0:1, 0:n]
        kind = iota((8, n), 0) & 3
        terms = []
        for r, field in enumerate((even_sum + odd_sum, even_dif + odd_dif,
                                   even_sum - odd_sum, even_dif - odd_dif)):
            square = field * field
            energy = 0.5 * (pltpu.roll(square, 7, 0) + pltpu.roll(square, 6, 0)) + pltpu.roll(field, 5, 0)
            flux = field * field[0:1]
            value = jnp.where(kind == 0, energy, jnp.where(kind == 3, 0.0, flux))
            value = jnp.where(inside, value, 0.0)
            terms_ref[r, :, cols] = value
            terms.append(value)
        even, odd = terms[0] + terms[2], terms[1] + terms[3]
        real, imag = terms[0] - terms[2], terms[1] - terms[3]
        folded = {0: even + odd, 2: even - odd}
        back = []
        for b in range(FINE):
            if b % 2 == 0:
                back.append(folded[b % 4] * turn_re[b])
            elif b % 4 == 1:
                back.append(real * turn_re[b] - imag * turn_im[b])
            else:
                back.append(real * turn_re[b] + imag * turn_im[b])
        g_hi, g_lo = split(jnp.concatenate(back, axis=0))
        both = dot(jnp.concatenate([g_hi, g_lo], axis=0), t_hi, NT)
        acc = acc + both[:128] + both[128:] + dot(g_hi, t_lo, NT)

    swapped = swap(acc[:, 128:])
    analysed = acc[:, :128] + jnp.where(in_real, swapped, -swapped)
    analysed = analysed * own_ref[1:2, 0:128]

    a_hi, a_lo = split(analysed)
    v = dot(jnp.concatenate([a_hi, a_lo], axis=1), jnp.concatenate([pick, pick], axis=0))
    for half in range(2):
        b_of = fine if half == 0 else FINE - 1 - fine
        cols = slice(order.shape[1] * half, order.shape[1] * (half + 1))
        xl = jnp.zeros((8, order.shape[1]), F32)
        for b in range(FINE):
            xl = xl + jnp.where(b_of == b, v[8 * b:8 * b + 8, cols], 0.0)
        pieces = []
        for i in range(5):
            pieces += [xl[:, 128 * i:128 * i + 128], jnp.zeros((8, 128), F32)]
        z = jnp.transpose(jnp.concatenate(pieces + [jnp.zeros((48, 128), F32)], axis=0))
        send_ref[:, half, :] = z[:64] + pltpu.roll(z[64:], 8, 1)


def layout_kernel(wave, owner_ref, points_ref, terms_ref, out_ref, line_ref):
    quarter = own_entry(owner_ref, points_ref, wave(), jnp.int32(0)) // 4
    line_ref[...] = jnp.zeros_like(line_ref)
    gap = jnp.zeros((8, 128), F32)
    for r in range(4):
        at = r * quarter
        value = jnp.concatenate([terms_ref[r], gap], axis=1)
        value = pltpu.roll(value, at % 128, 1)
        where = pl.ds(pl.multiple_of(at // 128 * 128, 128), QUARTER + 128)
        line_ref[:, where] = line_ref[:, where] + value
    for f in range(3):
        out_ref[0, f, 0:1, :] = line_ref[f:f + 1, 0:PMAX]


def parts_kernel(legendre_ref, after_ref, parts_ref):
    for p in range(parts_ref.shape[0]):
        parts_ref[p] = jnp.concatenate(split(legendre_ref[p]), axis=0)


def direct_kernel(wave, pairs, wt_ref, owner_ref, recv_ref, parts_ref, legendre_ref, out_ref,
                  v_ref, lg_ref, y_ref, sem, out_sem):
    me = wave()
    held = parts_ref.shape[0]
    copy = pltpu.make_async_copy(legendre_ref.at[pl.ds(held, pairs - held)], lg_ref, sem)
    copy.start()
    for j in range(owner_ref.shape[0]):
        source = owner_ref[j]
        for half in range(2):
            v_ref[half, j:j + 1, :] = recv_ref[source, half:half + 1, :]
    lane = iota((16, 128), 1)
    turned = [jnp.transpose(jnp.concatenate([v_ref[half], v_ref[half]], axis=0)) for half in range(2)]

    def one(p, rhs):
        bound = 1280 - wt_ref[me * pairs + p]
        q = jnp.concatenate([t[8 * p:8 * p + 8] for t in turned], axis=0)
        hi, lo = split(q)
        lhs = jnp.concatenate([hi, jnp.where(lane < 64, lo, jnp.zeros_like(lo))], axis=0)
        o = dot(lhs, rhs)
        o = o[:16] + o[16:]
        y = jnp.where(iota((8, o.shape[1]), 1) < bound, o[:8], o[8:])
        for f in range(3):
            y_ref[p, 0, f, 0:1, :] = y[f:f + 1]
            y_ref[p, 0, f, 1:2, :] = y[4 + f:5 + f]

    def leave(first, last, slot):
        at = pl.ds(first, last - first)
        out = pltpu.make_async_copy(y_ref.at[at], out_ref.at[at], out_sem.at[slot])
        out.start()
        return out

    for p in range(held):
        one(p, parts_ref[p])
    outs = [leave(0, held, 0)]
    copy.wait()
    for p in range(held, pairs):
        one(p, jnp.concatenate(split(lg_ref[p - held]), axis=0))
    outs.append(leave(held, pairs, 1))
    for out in outs:
        out.wait()


def params(megabytes=24):
    return pltpu.CompilerParams(vmem_limit_bytes=megabytes << 20)


def cost(us):
    return pl.CostEstimate(flops=int(us * 1e9), bytes_accessed=int(us * 3e6), transcendentals=0)


def run_legendre(wave, lev, levels, wave_table, factor, spectra, legendre):
    pairs, lat, slots = legendre.shape
    return pl.pallas_call(
        functools.partial(legendre_kernel, wave, lev, pairs, GROUPS),
        in_specs=[HBM, HBM, HBM, HBM],
        out_specs=[VMEM, VMEM],
        out_shape=[jax.ShapeDtypeStruct((2, 8 * pairs, 128), F32),
                   jax.ShapeDtypeStruct((levels, pairs, 2, 128), F32)],
        scratch_shapes=[pltpu.VMEM(spectra.shape, F32), pltpu.VMEM((pairs, 8, slots), F32),
                        pltpu.VMEM(legendre.shape, F32), pltpu.VMEM((pairs, 2, 128), F32),
                        pltpu.VMEM((1, 1), F32), pltpu.SMEM(wave_table.shape, jnp.int32),
                        pltpu.SemaphoreType.DMA((pairs + 3,))],
        compiler_params=params(56), cost_estimate=cost(3.0), name="legendre_inverse",
    )(wave_table, factor.reshape(1, 1), spectra, legendre)


def run_arrange(lat_owner, ft):
    return pl.pallas_call(
        arrange_kernel,
        in_specs=[SMEM, VMEM],
        out_specs=VMEM,
        out_shape=jax.ShapeDtypeStruct((2, lat_owner.shape[0], 128), F32),
        scratch_shapes=[pltpu.VMEM((2, 128, 128), F32), pltpu.VMEM((2, 128, 128), F32)],
        compiler_params=params(), cost_estimate=cost(1.0), name="arrange_rows",
    )(lat_owner, ft)


def run_gather(pairs, lat_owner, base, recv):
    return pl.pallas_call(
        functools.partial(gather_kernel, pairs),
        in_specs=[HBM, VMEM, VMEM],
        out_specs=VMEM,
        out_shape=jax.ShapeDtypeStruct((lat_owner.shape[0], 2, 128), F32),
        scratch_shapes=[pltpu.VMEM((pairs, 2, 128), F32), pltpu.VMEM((2, 128, 128), F32),
                        pltpu.VMEM((2, 128, 128), F32),
                        pltpu.SMEM(lat_owner.shape, jnp.int32), pltpu.SemaphoreType.DMA],
        compiler_params=params(), cost_estimate=cost(1.0), name="add_geopotential",
    )(lat_owner, base, recv)


def run_tables(wave, lat_owner, row_points, weights, order):
    return pl.pallas_call(
        functools.partial(table_kernel, wave),
        in_specs=[SMEM, SMEM, SMEM, VMEM],
        out_specs=[VMEM] * 6,
        out_shape=[jax.ShapeDtypeStruct((2 * COARSE, QUARTER), BF16)] * 2
        + [jax.ShapeDtypeStruct((FINE, QUARTER), F32)] * 2
        + [jax.ShapeDtypeStruct((8, 256), F32),
           jax.ShapeDtypeStruct((128, 2 * order.shape[1]), BF16)],
        compiler_params=params(), cost_estimate=cost(2.0), name="angle_tables",
    )(lat_owner, row_points, weights, order)


def run_grid(order, recv, tables):
    return pl.pallas_call(
        grid_kernel,
        in_specs=[VMEM] * 8,
        out_specs=[VMEM, VMEM],
        out_shape=[jax.ShapeDtypeStruct(recv.shape, F32),
                   jax.ShapeDtypeStruct((4, 8, QUARTER), F32)],
        compiler_params=params(), cost_estimate=cost(5.0), name="grid_space",
    )(order, recv, *tables)


def run_layout(wave, lat_owner, row_points, terms):
    return pl.pallas_call(
        functools.partial(layout_kernel, wave),
        in_specs=[SMEM, SMEM, VMEM],
        out_specs=VMEM,
        out_shape=jax.ShapeDtypeStruct((1, 3, 1, PMAX), F32),
        scratch_shapes=[pltpu.VMEM((8, 5504), F32)],
        compiler_params=params(), cost_estimate=cost(2.0), name="grid_terms",
    )(lat_owner, row_points, terms)


def run_parts(legendre, after):
    pairs, lat, slots = legendre.shape
    held = pairs * 9 // 10
    return pl.pallas_call(
        parts_kernel, in_specs=[VMEM, HBM], out_specs=VMEM,
        out_shape=jax.ShapeDtypeStruct((held, 2 * lat, slots), BF16),
        compiler_params=params(), cost_estimate=cost(1.0), name="legendre_parts",
    )(legendre, after)


def run_direct(wave, wave_table, lat_owner, recv, parts, legendre):
    pairs, lat, slots = legendre.shape
    return pl.pallas_call(
        functools.partial(direct_kernel, wave, pairs),
        in_specs=[SMEM, SMEM, VMEM, VMEM, HBM],
        out_specs=HBM,
        out_shape=jax.ShapeDtypeStruct((pairs, 1, 3, 2, slots), F32),
        scratch_shapes=[pltpu.VMEM((2, 64, 128), F32),
                        pltpu.VMEM((pairs - parts.shape[0], lat, slots), F32),
                        pltpu.VMEM((pairs, 1, 3, 2, slots), F32),
                        pltpu.SemaphoreType.DMA, pltpu.SemaphoreType.DMA((2,))],
        compiler_params=params(49), cost_estimate=cost(3.0), name="legendre_direct",
    )(wave_table, lat_owner, recv, parts, legendre)


def spectral_order(wave_table, waves):
    return jnp.transpose(wave_table.reshape(waves, -1)).reshape(1, -1)


def per_device(spectra, legendre, wave_table, lat_owner, row_points, weights, layer_depth_factor):
    waves, levels = lax.axis_size("wave"), lax.axis_size("lev")
    wave = functools.partial(lax.axis_index, "wave")
    lev = functools.partial(lax.axis_index, "lev")
    pairs = spectra.shape[0]
    ft, thick = run_legendre(wave, lev, levels, wave_table, layer_depth_factor, spectra, legendre)
    arrived = lax.all_to_all(thick, "lev", split_axis=0, concat_axis=0, tiled=True)
    order = spectral_order(wave_table, waves)
    tables = run_tables(wave, lat_owner, row_points, weights, order)
    outgoing = run_gather(pairs, lat_owner, run_arrange(lat_owner, ft), arrived)
    arrived = lax.all_to_all(outgoing, "wave", split_axis=0, concat_axis=0, tiled=True)
    outgoing, terms = run_grid(order, arrived, tables)
    arrived = lax.all_to_all(outgoing, "wave", split_axis=0, concat_axis=0, tiled=True)
    grid_terms = run_layout(wave, lat_owner, row_points, terms)
    parts = run_parts(legendre, terms)
    spectral_out = run_direct(wave, wave_table, lat_owner, arrived, parts, legendre)
    return spectral_out, jnp.transpose(grid_terms, (0, 2, 1, 3))


def solution(mesh):
    placed = (
        P("wave", "lev", None, None, None),
        P("wave", None, None),
        P(),
        P(),
        P(),
        P(),
        P("lev"),
    )
    return jax.shard_map(
        per_device,
        mesh=mesh,
        in_specs=placed,
        out_specs=(P("wave", "lev", None, None, None), P("wave", "lev", None, None)),
        check_vma=False,
    )
```
